32 devices in a mesh: dp: 4 (over y, x), mp: 8 (over z, core).
Axes of the slice: x: 2, y: 2, z: 4, core: 2. Of those that a mesh axis runs over, the one named last changes fastest.
Arguments:
- tokens: bfloat16 [3072, 16384], P('dp', 'mp'), may hold values from -6 to 6
- cotangent: bfloat16 [3072, 16384], P('dp', 'mp'), may hold values from -6 to 6
- blocks_w: bfloat16 [16, 5, 1024, 1024], P('mp'), may hold values from -0.078125 to 0.078125
- lowrank_u: bfloat16 [16384, 256], P('mp'), may hold values from -0.046875 to 0.046875
- lowrank_v: bfloat16 [256, 16384], P(None, 'mp'), may hold values from -0.375 to 0.375
Outputs:
- grad_tokens: float32 [3072, 16384], P('dp', 'mp')
- grad_blocks: float32 [1024, 16, 5, 1024], P('dp', 'mp')
- grad_u: float32 [16384, 256], P(('mp', 'dp'))
- grad_v: float32 [256, 16384], P(None, ('mp', 'dp'))
The draws below stay inside these ranges and needn't reach their ends.
All inputs are finite; a program needn't handle non-finite values.
Results may differ from the reference program's by a relative error of at most 0.0029.
Values may be sent and summed in bfloat16 or wider, within the bound.
No kernel may reach another device: no remote copies, remote signals or barrier semaphores. Data moves between devices by JAX's collectives and lax.ppermute only.
A program may use at most 192 MiB of HBM per device.

```python
import math
import jax
import jax.numpy as jnp
from jax import lax

NB = 16
BLK = 1024
R = 256
TOK_DEV = 768
SLOTS = 5
D = 16384
TOKENS = 3072
N_DP = 4


def level_of(own_key, dims, cuts, smallest, high):
    gain, own = 1.0, jax.random.fold_in(own_key, 6)
    for axis_at, parts in cuts:
        heights = jnp.exp(jax.random.uniform(jax.random.fold_in(own, axis_at), (parts,), jnp.float32, smallest / len(cuts), high / len(cuts)))
        gain = gain * jnp.repeat(heights, dims[axis_at] // parts).reshape([-1 if axis == axis_at else 1 for axis in range(len(dims))])
    return gain


def bell_draw(own_key, extent, deviation, most, pieces=(), kind=jnp.bfloat16):
    array = jax.random.normal(own_key, extent, jnp.float32) * deviation
    if len(pieces) > 0:
        array = level_of(own_key, extent, pieces, -0.22, 0.18) * array
    return jnp.clip(array, min=-most, max=most).astype(kind)


def setup_inputs(seed: int = 0) -> dict:
    key_of = jax.random.split(jax.random.key(seed), 6)
    tokens = bell_draw(key_of[0], (TOKENS, D), 1.0, 6.0, ((0, 4), (1, 8)))
    cotangent = bell_draw(key_of[1], (TOKENS, D), 1.0, 6.0, ((0, 4), (1, 8)))
    blocks_w = bell_draw(key_of[2], (NB, SLOTS, BLK, BLK), (SLOTS * BLK) ** -0.5, 0.078125, ((0, 8),))
    lowrank_u = bell_draw(key_of[3], (D, R), D ** -0.5, 0.046875, ((0, 8),))
    lowrank_v = bell_draw(key_of[4], (R, D), R ** -0.5, 0.375, ((1, 8),))
    return {"tokens": tokens, "cotangent": cotangent, "blocks_w": blocks_w, "lowrank_u": lowrank_u, "lowrank_v": lowrank_v}


def source_block(block, slot):
    if slot == 0:
        return block
    return block ^ 1 << slot - 1

def reference(tokens, cotangent, blocks_w, lowrank_u, lowrank_v):
    grad_scale = 1.0 / math.sqrt(TOKENS)
    tok_blocks = tokens.reshape(TOKENS, NB, BLK)
    cot_blocks = cotangent.reshape(TOKENS, NB, BLK)
    low_in = jnp.dot(tokens, lowrank_u, preferred_element_type=jnp.float32).astype(jnp.bfloat16)
    low_back = jnp.dot(cotangent, lowrank_v.T, preferred_element_type=jnp.float32).astype(jnp.bfloat16)
    back_low = jnp.dot(low_back, lowrank_u.T, preferred_element_type=jnp.float32)
    columns = []
    for block in range(NB):
        total = back_low[:, block * BLK:(block + 1) * BLK]
        for slot in range(SLOTS):
            other = source_block(block, slot)
            total = total + jnp.dot(cot_blocks[:, other], blocks_w[other, slot].T, preferred_element_type=jnp.float32)
        columns.append(total)
    grad_tokens = jnp.concatenate(columns, axis=1)
    grads = []
    for block in range(NB):
        cot_shards = cot_blocks[:, block].reshape(N_DP, TOK_DEV, BLK).astype(jnp.float32)
        slot_grads = []
        for slot in range(SLOTS):
            tok_shards = tok_blocks[:, source_block(block, slot)].reshape(N_DP, TOK_DEV, BLK).astype(jnp.float32)
            partial_value = jnp.einsum('nti,nto->nio', tok_shards, cot_shards)
            slot_grads.append(lax.optimization_barrier(jnp.sum(partial_value, axis=0)) * grad_scale)
        grads.append(jnp.stack(slot_grads, axis=1))
    grad_blocks = jnp.stack(grads, axis=1)
    grad_u = jnp.dot(tokens.T, low_back, preferred_element_type=jnp.float32) * grad_scale
    grad_v = jnp.dot(low_in.T, cotangent, preferred_element_type=jnp.float32) * grad_scale
    return (grad_tokens, grad_blocks, grad_u, grad_v)
```

```python
import math

import jax
import jax.numpy as jnp
from jax import lax
from jax.experimental import pallas as pl
from jax.experimental.pallas import tpu as pltpu
from jax.sharding import PartitionSpec as P

F32 = jnp.float32
BF16 = jnp.bfloat16
ROOM = 56 * 1024 * 1024
QUICK = pl.CostEstimate(flops=0, bytes_accessed=0, transcendentals=0)


def swap(value, axis, apart):
    count = lax.axis_size(axis)
    return lax.ppermute(value, axis, [(i, i ^ apart) for i in range(count)])


def tie(values, *others):
    return lax.optimization_barrier((values, others))[0]


def dot(a, b, dims):
    return lax.dot_general(a, b, (dims, ((), ())), preferred_element_type=F32)


def ordered(mine, theirs, bit, axis):
    return jnp.where(
        bit == 0,
        jnp.concatenate([mine, theirs], axis),
        jnp.concatenate([theirs, mine], axis),
    )


def call(body, **kwargs):
    return pl.pallas_call(
        body,
        compiler_params=pltpu.CompilerParams(vmem_limit_bytes=ROOM),
        cost_estimate=QUICK,
        **kwargs,
    )


def partner_term(cot, weights, slot, first_row, rows):
    blocks, _, width = weights.shape[:3]

    def body(c, w, o):
        o[...] = dot(c[...], w[0, 0], ((1,), (1,))).astype(BF16)

    start = first_row // rows
    return call(
        body,
        grid=(blocks,),
        in_specs=[
            pl.BlockSpec((rows, width), lambda j: (start, j)),
            pl.BlockSpec((1, 1, width, width), lambda j: (j, slot, 0, 0)),
        ],
        out_specs=pl.BlockSpec((rows, width), lambda j: (0, j)),
        out_shape=jax.ShapeDtypeStruct((rows, blocks * width), BF16),
    )(cot, weights)


def own_terms(cot, weights, count):
    blocks, _, width = weights.shape[:3]
    rows = cot.shape[0]
    tile = width // 2
    tiles = width // tile

    def body(c, *refs):
        o = refs[-1]
        for block in range(blocks):

            @pl.when(pl.program_id(0) == block)
            def _():
                value = None
                for s in range(count):
                    other = block ^ ((1 << s) >> 1)
                    more = dot(c[:, other * width : (other + 1) * width], refs[s][0, 0], ((1,), (1,)))
                    value = more if value is None else value + more
                o[...] = value

    def weight(s):
        return pl.BlockSpec(
            (1, 1, tile, width), lambda i, t: (i ^ ((1 << s) >> 1), s, t, 0)
        )

    return call(
        body,
        grid=(blocks, tiles),
        in_specs=[pl.BlockSpec((rows, blocks * width), lambda i, t: (0, 0))]
        + [weight(s) for s in range(count)],
        out_specs=pl.BlockSpec((rows, tile), lambda i, t: (0, i * tiles + t)),
        out_shape=jax.ShapeDtypeStruct((rows, blocks * width), F32),
    )(cot, *[weights] * count)


def turned_pieces(me, tokens, blocks, count):
    rows = tokens.shape[0]
    part = tokens.shape[1] // blocks // count

    def body(me_ref, *refs):
        for x in range(count):
            refs[count + x][...] = refs[x][...].T

    def columns(x):
        return pl.BlockSpec((rows, part), lambda j, me_ref: (0, j * count + (me_ref[0] ^ x)))

    return call(
        body,
        grid_spec=pltpu.PrefetchScalarGridSpec(
            num_scalar_prefetch=1,
            grid=(blocks,),
            in_specs=[columns(x) for x in range(count)],
            out_specs=[pl.BlockSpec((part, rows), lambda j, me_ref: (j, 0)) for _ in range(count)],
        ),
        out_shape=[jax.ShapeDtypeStruct((blocks * part, rows), BF16) for _ in range(count)],
    )(me, *[tokens] * count)


def row_parts(refs, which, first, count):
    found, at = [], 0
    for ref in refs:
        low, high = max(first, at), min(first + count, at + ref.shape[1])
        if low < high:
            found.append(ref[which, low - at : high - at, :])
        at += ref.shape[1]
    return found


def products(sources, cots, blocks):
    total = None
    for x, start, c in cots:
        lhs = []
        for refs, block in sources:
            part = sum(r.shape[1] for r in refs) // blocks
            lhs += row_parts(refs, x, block * part, part)
        lhs = jnp.concatenate(lhs, 0) if len(lhs) > 1 else lhs[0]
        if c.shape[0] != lhs.shape[1]:
            lhs = lhs[:, start : start + c.shape[0]]
        more = dot(lhs, c[...], ((1,), (0,)))
        total = more if total is None else total + more
    return total


def grouped(refs, groups):
    found = []
    for group in groups:
        found.append(refs[: len(group)])
        refs = refs[len(group) :]
    return found, refs


def early_grads(turned, near, cots, local, blocks, scale):
    part = sum(p.shape[1] for p in turned) // blocks
    width = cots[0][2].shape[1] // blocks
    tile = width // 2
    tiles = width // tile
    count = local + len(near)
    groups = [turned] + near
    pieces = [p for group in groups for p in group]

    def body(*refs):
        held, refs = grouped(refs, groups)
        mine = [(x, start, ref) for (x, start, _), ref in zip(cots, refs)]
        o = refs[-1]
        for block in range(blocks):

            @pl.when(pl.program_id(0) == block)
            def _():
                sources = [(held[0], block ^ ((1 << s) >> 1)) for s in range(local)]
                sources += [(refs_, block) for refs_ in held[1:]]
                value = products(sources, mine, blocks) * scale
                for s in range(count):
                    o[s, 0] = value[s * part : (s + 1) * part]

    return call(
        body,
        grid=(blocks, tiles),
        in_specs=[pl.BlockSpec(p.shape, lambda j, t: (0, 0, 0)) for p in pieces]
        + [pl.BlockSpec((c.shape[0], tile), lambda j, t: (0, j * tiles + t)) for _, _, c in cots],
        out_specs=pl.BlockSpec((count, 1, part, tile), lambda j, t: (0, j, 0, t)),
        out_shape=jax.ShapeDtypeStruct((count, blocks, part, width), F32),
    )(*pieces, *[c for _, _, c in cots])


def all_grads(early, far, cots, blocks, scale):
    count, _, part, width = early.shape
    slots = count + len(far)
    tile = width // 4
    tiles = width // tile
    pieces = [p for group in far for p in group]

    def body(e, *refs):
        held, refs = grouped(refs, far)
        o = refs[-1]
        for block in range(blocks):
            columns = refs[block * len(cots) : (block + 1) * len(cots)]
            mine = [(x, start, ref) for (x, start, _), ref in zip(cots, columns)]
            value = products([(group, block) for group in held], mine, blocks) * scale
            for s in range(count):
                o[:, s, block, :] = e[s, block]
            for k in range(len(far)):
                o[:, count + k, block, :] = value[k * part : (k + 1) * part]

    def columns(c, block):
        return pl.BlockSpec((c.shape[0], tile), lambda t: (0, block * tiles + t))

    out = call(
        body,
        grid=(tiles,),
        in_specs=[pl.BlockSpec((count, blocks, part, tile), lambda t: (0, 0, 0, t))]
        + [pl.BlockSpec(p.shape, lambda t: (0, 0, 0)) for p in pieces]
        + [columns(c, block) for block in range(blocks) for _, _, c in cots],
        out_specs=pl.BlockSpec((part, slots, blocks, tile), lambda t: (0, 0, 0, t)),
        out_shape=jax.ShapeDtypeStruct((part, slots, blocks, width), F32),
    )(early, *pieces, *[c for _, _, c in cots] * blocks)
    return jnp.transpose(out, (0, 2, 1, 3))


def halving(terms, orders):
    count = lax.axis_size("dp")
    me = lax.axis_index("dp")
    parts = []
    for term, axis in terms:
        size = term.shape[axis] // count
        parts.append(
            {x: lax.dynamic_slice_in_dim(term, (me ^ x) * size, size, axis) for x in range(count)}
        )
    for bits in zip(*orders):
        away = [sorted(x for x in p if x >> bit & 1) for p, bit in zip(parts, bits)]
        sent = [jnp.stack([p[x] for x in xs]) for p, xs in zip(parts, away)]
        sent = yield sent
        got = [swap(s, "dp", 1 << bit) for s, bit in zip(sent, bits)]
        got = yield got
        for p, xs, bit, g in zip(parts, away, bits, got):
            for at, x in enumerate(xs):
                p[x ^ 1 << bit] = p[x ^ 1 << bit] + g[at]
                del p[x]
    yield [p[0] for p in parts]


def per_device(tokens, cotangent, blocks_w, lowrank_u, lowrank_v):
    lb, slots, bw = blocks_w.shape[:3]
    rows = tokens.shape[0]
    n_dp = lax.axis_size("dp")
    dp_me = lax.axis_index("dp")
    part = bw // n_dp
    grad_scale = 1.0 / math.sqrt(rows * n_dp)
    bits = range(n_dp.bit_length() - 1)

    local = [s for s in range(1, slots) if 1 << (s - 1) < lb]
    remote = {s: (1 << (s - 1)) // lb for s in range(1, slots) if 1 << (s - 1) >= lb}
    near = [s for s in remote if remote[s] == 1]
    far = [s for s in remote if remote[s] > 1]
    mp_bits = lax.axis_size("mp").bit_length() - 1
    mp_me = lax.axis_index("mp")
    core, side = mp_me & 1, mp_me >> 1 & 1
    half = cut = rows // 2

    low = dot(tokens, lowrank_u, ((1,), (0,)))
    back = dot(cotangent, lowrank_v, ((1,), (1,)))
    kept = jnp.where(core == 0, low, back)
    sent = jnp.where(core == 0, back, low)
    got = swap(sent, "mp", 1)

    cot1 = tie(cotangent, kept, sent)
    first = {}
    for s in far[::-1]:
        first[s] = partner_term(cot1, blocks_w, s, 0, cut)
        cot1 = tie(cot1, first[s])
    first_in = {s: swap(first[s], "mp", remote[s]) for s in far}

    kept = kept + tie(got, cot1)
    sent = lax.dynamic_slice_in_dim(kept, (1 - side) * half, half, 0)
    kept = lax.dynamic_slice_in_dim(kept, side * half, half, 0)
    got = swap(sent, "mp", 2)

    tokens1 = tie(tokens, kept, sent)
    me = jnp.reshape(dp_me, (1,)).astype(jnp.int32)
    turned = turned_pieces(me, tokens1, lb, n_dp)
    turned, got, cot1 = tie((turned, got, cot1))
    turned = [turned[0]] + [swap(turned[x], "dp", x) for x in range(1, n_dp)]
    kept = kept + got

    near_out = {s: partner_term(cot1, blocks_w, s, 0, rows) for s in near}
    cot1 = tie(cot1, near_out)
    base = own_terms(cot1, blocks_w, 1 + len(local))
    cot1 = tie(cot1, base)
    second = {s: partner_term(cot1, blocks_w, s, cut, rows - cut) for s in far}

    turned, kept = tie((turned, kept), second)
    got = swap(kept, "mp", 4)
    middle = lb * part // 2
    turned = (
        jnp.stack([t[:middle] for t in turned]),
        jnp.stack([t[middle:] for t in turned]),
    )

    first_in, turned, got, second, cot1 = tie((first_in, turned, got, second, cotangent))
    far_a = {s: swap(turned[0], "mp", remote[s]) for s in far}
    if n_dp == 4:
        c1, c2 = swap(cot1, "dp", 1), swap(cot1, "dp", 2)
    else:
        cots = [(x, 0, swap(cot1, "dp", x) if x else cotangent) for x in range(n_dp)]
    kept = kept + got
    for bit in range(3, mp_bits):
        kept = kept + swap(kept, "mp", 1 << bit)
    kept = kept.astype(BF16)
    got = swap(kept, "mp", 2)

    if n_dp == 4:
        far_a, got, second_half, c1, c2 = tie((far_a, got, turned[1], c1, c2))
    else:
        far_a, got, second_half = tie((far_a, got, turned[1]))
    far_b = {s: swap(second_half, "mp", remote[s]) for s in far}
    if n_dp == 4:
        c3a = swap(c1[:half], "dp", 2)
        c3b = swap(c2[half:], "dp", 1)
        cots = [(0, 0, cotangent), (1, 0, c1), (2, 0, c2), (3, 0, c3a), (3, half, c3b)]
    whole = ordered(kept, got, side, 0)
    other = swap(whole, "mp", 1)
    low_in = jnp.where(core == 0, whole, other)
    low_back = jnp.where(core == 0, other, whole)
    near_tok = []
    for s in near:
        a = swap(tie(turned[0], low_in, low_back), "mp", remote[s])
        near_tok.append((a, swap(tie(turned[1], a), "mp", remote[s])))
    near_out = tie(near_out, near_tok)
    near_in = {s: swap(near_out[s], "mp", remote[s]) for s in near}

    sums = halving(
        [
            (dot(tokens, low_back, ((0,), (0,))), 0),
            (dot(low_in, cotangent, ((0,), (0,))), 1),
        ],
        [list(bits), list(bits)[::-1]],
    )
    out = next(sums)
    full = base + dot(low_back, lowrank_u, ((1,), (1,)))
    for s in near:
        full = full + near_in[s].astype(F32)
    head = full[:cut]
    for s in far:
        head = head + first_in[s].astype(F32)
    full = lax.dynamic_update_slice(full, head, (0, 0))
    early = early_grads(turned, near_tok, cots, 1 + len(local), lb, grad_scale)

    far_b, second, early, out, full = tie((far_b, second, early, out, full))
    second_in = {s: swap(second[s], "mp", remote[s]) for s in far}
    for step in bits:
        out = sums.send(sums.send(out))
    grad_u, grad_v = out[0] * grad_scale, out[1] * grad_scale
    grad_blocks = all_grads(early, [(far_a[s], far_b[s]) for s in far], cots, lb, grad_scale)

    second_in, full = tie((second_in, full), grad_blocks, grad_u, grad_v)
    tail = full[cut:]
    for s in far:
        tail = tail + second_in[s].astype(F32)
    grad_tokens = lax.dynamic_update_slice(full, tail, (cut, 0))
    return (grad_tokens, grad_blocks, grad_u, grad_v)


def solution(mesh):
    in_specs = (
        P("dp", "mp"),
        P("dp", "mp"),
        P("mp", None, None, None),
        P("mp", None),
        P(None, "mp"),
    )
    out_specs = (
        P("dp", "mp"),
        P("dp", "mp", None, None),
        P(("mp", "dp"), None),
        P(None, ("mp", "dp")),
    )
    return jax.shard_map(
        per_device, mesh=mesh, in_specs=in_specs, out_specs=out_specs, check_vma=False
    )
```

```python
import math

import jax
import jax.numpy as jnp
from jax import lax
from jax.experimental import pallas as pl
from jax.experimental.pallas import tpu as pltpu
from jax.sharding import PartitionSpec as P

F32 = jnp.float32
BF16 = jnp.bfloat16
ROOM = 56 * 1024 * 1024
QUICK = pl.CostEstimate(flops=0, bytes_accessed=0, transcendentals=0)
GATHER = (2, 1)
REDUCE = (1, 2)


def swap(value, axis, apart):
    count = lax.axis_size(axis)
    return lax.ppermute(value, axis, [(i, i ^ apart) for i in range(count)])


def tie(values, *others):
    return lax.optimization_barrier((values, others))[0]


def dot(a, b, dims):
    return lax.dot_general(a, b, (dims, ((), ())), preferred_element_type=F32)


def ordered(mine, theirs, bit, axis):
    return jnp.where(
        bit == 0,
        jnp.concatenate([mine, theirs], axis),
        jnp.concatenate([theirs, mine], axis),
    )


def call(body, **kwargs):
    return pl.pallas_call(
        body,
        compiler_params=pltpu.CompilerParams(vmem_limit_bytes=ROOM),
        cost_estimate=QUICK,
        **kwargs,
    )


def prefetched(body, me, grid, in_specs, out_specs, out_shape, operands, **kwargs):
    spec = pltpu.PrefetchScalarGridSpec(
        num_scalar_prefetch=1, grid=grid, in_specs=in_specs, out_specs=out_specs
    )
    return call(body, grid_spec=spec, out_shape=out_shape, **kwargs)(me, *operands)


def partner_term(cot, weights, slot):
    blocks, _, width = weights.shape[:3]
    rows = cot.shape[0]

    def body(c, w, o):
        o[...] = dot(c[...], w[0, 0], ((1,), (1,))).astype(BF16)

    return call(
        body,
        grid=(blocks,),
        in_specs=[
            pl.BlockSpec((rows, width), lambda j: (0, j)),
            pl.BlockSpec((1, 1, width, width), lambda j: (j, slot, 0, 0)),
        ],
        out_specs=pl.BlockSpec((rows, width), lambda j: (0, j)),
        out_shape=jax.ShapeDtypeStruct((rows, blocks * width), BF16),
    )(cot, weights)


def own_terms(cot, weights, count):
    blocks, _, width = weights.shape[:3]
    rows = cot.shape[0]
    tile = width // 2
    tiles = width // tile

    def body(c, *refs):
        o = refs[-1]
        for block in range(blocks):

            @pl.when(pl.program_id(0) == block)
            def _():
                value = None
                for s in range(count):
                    other = block ^ ((1 << s) >> 1)
                    more = dot(c[:, other * width : (other + 1) * width], refs[s][0, 0], ((1,), (1,)))
                    value = more if value is None else value + more
                o[...] = value

    def weight(s):
        return pl.BlockSpec((1, 1, tile, width), lambda i, t: (i ^ ((1 << s) >> 1), s, t, 0))

    return call(
        body,
        grid=(blocks, tiles),
        in_specs=[pl.BlockSpec((rows, blocks * width), lambda i, t: (0, 0))]
        + [weight(s) for s in range(count)],
        out_specs=pl.BlockSpec((rows, tile), lambda i, t: (0, i * tiles + t)),
        out_shape=jax.ShapeDtypeStruct((rows, blocks * width), F32),
    )(cot, *[weights] * count)


def projections(core, tokens, cot, u, v):
    rows, width = tokens.shape
    rank = u.shape[1]
    tile = rows // 2

    def body(core_ref, t, c, u_ref, v_ref, kept, sent):
        low = dot(t[...], u_ref[...], ((1,), (0,)))
        back = dot(c[...], v_ref[...], ((1,), (1,)))
        first = core_ref[0] == 0
        kept[...] = jnp.where(first, low, back)
        sent[...] = jnp.where(first, back, low)

    shape = jax.ShapeDtypeStruct((rows, rank), F32)
    return call(
        body,
        grid=(rows // tile,),
        in_specs=[
            pl.BlockSpec(memory_space=pltpu.SMEM),
            pl.BlockSpec((tile, width), lambda r: (r, 0)),
            pl.BlockSpec((tile, width), lambda r: (r, 0)),
            pl.BlockSpec((width, rank), lambda r: (0, 0)),
            pl.BlockSpec((rank, width), lambda r: (0, 0)),
        ],
        out_specs=[pl.BlockSpec((tile, rank), lambda r: (r, 0))] * 2,
        out_shape=[shape, shape],
    )(core, tokens, cot, u, v)


def pieces(me, tokens, cot, blocks, part):
    rows, width = tokens.shape
    width //= blocks
    tile = rows // 3

    def body(me_ref, t, c, held, *given):
        def shard(block, x):
            start = pl.multiple_of(block * width + (me_ref[0] ^ x) * part, part)
            return t[:, pl.ds(start, part)]

        for j in range(blocks):
            held[:, 2 * j * part : (2 * j + 1) * part] = shard(j, 0)
            held[:, (2 * j + 1) * part : (2 * j + 2) * part] = shard(j, REDUCE[j])
            for at, block in enumerate((j, j ^ 1)):
                start = 2 * at * part
                given[j][:, start : start + part] = shard(block, GATHER[j])
                given[j][:, start + part : start + 2 * part] = shard(block, GATHER[j] ^ REDUCE[j])
            given[j][:, 4 * part :] = c[:, j * width : (j + 1) * width]

    widths = [2 * blocks * part] + [4 * part + width] * blocks
    return prefetched(
        body,
        me,
        (rows // tile,),
        [pl.BlockSpec((tile, blocks * width), lambda r, m: (r, 0))] * 2,
        [pl.BlockSpec((tile, w), lambda r, m: (r, 0)) for w in widths],
        [jax.ShapeDtypeStruct((rows, w), BF16) for w in widths],
        (tokens, cot),
    )


def slot_sums(me, j, tokens, cot, given, local, partners, part):
    rows = tokens.shape[0]
    width = given.shape[1] - 4 * part
    shards = width // part
    slots = 2 * local + len(partners)
    tile = width // 2
    mine = 4 * local

    def body(me_ref, *refs):
        far = refs[mine + 2 * local : -4]
        c0, c1, kept, sent = refs[-4:]
        first = list(refs[:mine]) + list(far[0::2])
        second = list(refs[mine : mine + 2 * local]) + list(far[1::2])
        value = dot(jnp.concatenate([r[...] for r in first], 1), c0[...], ((0,), (0,)))
        value = value + dot(jnp.concatenate([r[...] for r in second], 1), c1[...], ((0,), (0,)))
        for s in range(slots):
            kept[s] = value[2 * s * part : (2 * s + 1) * part]
            sent[s] = value[(2 * s + 1) * part : (2 * s + 2) * part].astype(BF16)

    def shard(block, x):
        return pl.BlockSpec((rows, part), lambda t, m: (0, block * shards + (m[0] ^ x)))

    def pair(at):
        return pl.BlockSpec((rows, 2 * part), lambda t, m: (0, at))

    in_specs, operands = [], []
    if local:
        in_specs += [shard(j, 0), shard(j, REDUCE[j]), shard(j ^ 1, 0), shard(j ^ 1, REDUCE[j])]
        in_specs += [pair(0), pair(1)]
        operands += [tokens] * 4 + [given] * 2
    for one, two in partners:
        in_specs += [pair(one[1]), pair(two[1])]
        operands += [one[0], two[0]]
    in_specs += [
        pl.BlockSpec((rows, tile), lambda t, m: (0, j * (width // tile) + t)),
        pl.BlockSpec((rows, tile), lambda t, m: (0, 4 * part // tile + t)),
    ]
    out = pl.BlockSpec((slots, part, tile), lambda t, m: (0, 0, t))
    shape = (slots, part, width)
    return prefetched(
        body,
        me,
        (width // tile,),
        in_specs,
        [out, out],
        [jax.ShapeDtypeStruct(shape, F32), jax.ShapeDtypeStruct(shape, BF16)],
        (*operands, cot, given),
    )


def all_grads(kept, got, scale):
    blocks = len(kept)
    counts = [k.shape[0] for k in kept[0]]
    _, part, width = kept[0][0].shape
    slots = sum(counts)
    tile = width // 4

    def body(*refs):
        o = refs[-1]
        refs = iter(refs)
        for j in range(blocks):
            at = 0
            for count in counts:
                mine, theirs = next(refs), next(refs)
                for s in range(count):
                    o[:, at + s, j, :] = (mine[s] + theirs[s].astype(F32)) * scale
                at += count

    operands = [
        x for j in range(blocks) for pair in zip(kept[j], got[j]) for x in pair
    ]
    out = call(
        body,
        grid=(width // tile,),
        in_specs=[pl.BlockSpec((x.shape[0], part, tile), lambda t: (0, 0, t)) for x in operands],
        out_specs=pl.BlockSpec((part, slots, blocks, tile), lambda t: (0, 0, 0, t)),
        out_shape=jax.ShapeDtypeStruct((part, slots, blocks, width), F32),
    )(*operands)
    return jnp.transpose(out, (0, 2, 1, 3))


def joined(base, near, low_back, u):
    rows, width = base.shape
    tile = width // 4

    def body(b, n, l, u_ref, o):
        o[...] = b[...] + n[...].astype(F32) + dot(l[...], u_ref[...], ((1,), (1,)))

    block = pl.BlockSpec((rows, tile), lambda t: (0, t))
    return call(
        body,
        grid=(width // tile,),
        in_specs=[
            block,
            block,
            pl.BlockSpec(low_back.shape, lambda t: (0, 0)),
            pl.BlockSpec((tile, u.shape[1]), lambda t: (t, 0)),
        ],
        out_specs=block,
        out_shape=jax.ShapeDtypeStruct(base.shape, F32),
    )(base, near, low_back, u)


def added(base, *terms):
    rows, width = base.shape
    tile = rows // 6

    def body(b, *refs):
        value = b[...]
        for ref in refs[:-1]:
            value = value + ref[...].astype(F32)
        refs[-1][...] = value

    block = pl.BlockSpec((tile, width), lambda r: (r, 0))
    return call(
        body,
        grid=(rows // tile,),
        in_specs=[block] * (1 + len(terms)),
        out_specs=block,
        out_shape=jax.ShapeDtypeStruct(base.shape, F32),
        input_output_aliases={0: 0},
    )(base, *terms)


def summed_rows(term):
    me = lax.axis_index("dp")
    size = term.shape[0] // 4
    parts = [lax.dynamic_slice_in_dim(term, (me ^ x) * size, size, 0) for x in range(4)]
    got = swap(jnp.concatenate([parts[1], parts[3]], 0).astype(BF16), "dp", 1).astype(F32)
    mine, theirs = parts[0] + got[:size], parts[2] + got[size:]
    return mine + swap(theirs.astype(BF16), "dp", 2).astype(F32)


def square(tokens, cotangent, blocks_w, lowrank_u, lowrank_v):
    lb, slots, bw = blocks_w.shape[:3]
    rows = tokens.shape[0]
    n_dp = lax.axis_size("dp")
    part = bw // n_dp
    scale = 1.0 / math.sqrt(rows * n_dp)
    me = jnp.reshape(lax.axis_index("dp"), (1,)).astype(jnp.int32)
    mp_me = lax.axis_index("mp")
    core, side = mp_me & 1, mp_me >> 1 & 1
    half = rows // 2
    near, far = 2, (3, 4)
    apart = {s: (1 << (s - 1)) // lb for s in (near, *far)}

    held, *given = pieces(me, tokens, cotangent, lb, part)
    given = [swap(g, "dp", GATHER[j]) for j, g in enumerate(given)]
    held_in = {s: swap(held, "mp", apart[s]) for s in far}

    tokens1, cot1 = tie((tokens, cotangent), held)
    kept, sent = projections(
        jnp.reshape(core, (1,)).astype(jnp.int32), tokens1, cot1, lowrank_u, lowrank_v
    )
    got = swap(sent, "mp", 1)
    cot1 = tie(cot1, kept)
    out = {near: partner_term(cot1, blocks_w, near)}
    kept = kept + tie(got, out)
    for s in far:
        cot1 = tie(cot1, out)
        out[s] = partner_term(cot1, blocks_w, s)
    base = own_terms(tie(cot1, out), blocks_w, 2)
    kept = tie(kept, base)
    sent = lax.dynamic_slice_in_dim(kept, (1 - side) * half, half, 0)
    kept = lax.dynamic_slice_in_dim(kept, side * half, half, 0)
    got = swap(sent, "mp", 2)

    given, held_in, out, got = tie((given, held_in, out, got), base)
    more = jnp.concatenate([given[j][:, : 2 * part] for j in range(lb)], 1)
    more_in = {s: swap(more, "mp", apart[s]) for s in far}
    near_tok = swap(jnp.concatenate([held, more], 1), "mp", apart[near])
    near_in = swap(out[near], "mp", apart[near])
    kept = kept + got
    got = swap(kept, "mp", 4)

    kept = (kept + got).astype(BF16)
    got = swap(kept, "mp", 2)
    whole = ordered(kept, got, side, 0)
    other = swap(whole, "mp", 1)
    low_in = jnp.where(core == 0, whole, other)
    low_back = jnp.where(core == 0, other, whole)

    out = tie(out, near_tok, near_in)
    far_in = [swap(out[s], "mp", apart[s]) for s in far]

    sums = [
        slot_sums(
            me,
            j,
            tokens,
            cotangent,
            given[j],
            True,
            [((near_tok, j), (near_tok, lb + j))] + [((held_in[s], j), (more_in[s], j)) for s in far],
            part,
        )
        for j in range(lb)
    ]
    sums_in = [swap(sums[j][1], "dp", REDUCE[j]) for j in range(lb)]

    u_term = dot(tokens, low_back, ((0,), (0,)))
    v_term = dot(cotangent, low_in, ((0,), (0,)))
    uv = summed_rows(jnp.concatenate([u_term, v_term], 1)) * scale
    rank = lowrank_u.shape[1]
    grad_u, grad_v = uv[:, :rank], uv[:, rank:].T
    full = joined(base, near_in, low_back, lowrank_u)
    sums_in = tie(sums_in, full)
    grad_blocks = all_grads([[s[0]] for s in sums], [[s] for s in sums_in], scale)
    far_in, full = tie((far_in, full), grad_blocks)
    return (added(full, *far_in), grad_blocks, grad_u, grad_v)


def general(tokens, cotangent, blocks_w, lowrank_u, lowrank_v):
    lb, slots, bw = blocks_w.shape[:3]
    rows = tokens.shape[0]
    n_dp = lax.axis_size("dp")
    part = bw // n_dp
    scale = 1.0 / math.sqrt(rows * n_dp)

    def blocks_of(value):
        return value.reshape(value.shape[0], lb, -1)

    def partner(value, slot):
        distance = (1 << slot) >> 1
        if distance < lb:
            return jnp.stack([value[:, j ^ distance] for j in range(lb)], 1)
        return swap(value, "mp", distance // lb)

    low = dot(tokens, lowrank_u, ((1,), (0,)))
    back = dot(cotangent, lowrank_v, ((1,), (1,)))
    low, back = lax.psum((low, back), "mp")
    low, back = low.astype(BF16), back.astype(BF16)

    turned = tokens.reshape(rows, lb, n_dp, part)
    turned = lax.all_to_all(turned, "dp", 2, 0, tiled=True).reshape(n_dp * rows, lb, part)
    cot_all = blocks_of(lax.all_gather(cotangent, "dp", tiled=True))
    cot = blocks_of(cotangent)
    total = blocks_of(dot(back, lowrank_u, ((1,), (1,))))
    grads = []
    for s in range(slots):
        term = jnp.einsum("tbo,bio->tbi", cot, blocks_w[:, s], preferred_element_type=F32)
        if (1 << s) >> 1 >= lb:
            term = term.astype(BF16)
        total = total + partner(term, s).astype(F32)
        grads.append(
            jnp.einsum("tbi,tbo->ibo", partner(turned, s), cot_all, preferred_element_type=F32)
        )
    grad_blocks = jnp.stack(grads, 2) * scale
    u_term = dot(tokens, back, ((0,), (0,)))
    v_term = dot(low, cotangent, ((0,), (0,)))
    grad_u = lax.psum_scatter(u_term, "dp", scatter_dimension=0, tiled=True)
    grad_v = lax.psum_scatter(v_term, "dp", scatter_dimension=1, tiled=True)
    return (total.reshape(rows, lb * bw), grad_blocks, grad_u * scale, grad_v * scale)


def per_device(tokens, cotangent, blocks_w, lowrank_u, lowrank_v):
    sizes = (blocks_w.shape[0], lax.axis_size("dp"), lax.axis_size("mp"))
    plan = square if sizes == (2, 4, 8) and blocks_w.shape[1] == 5 else general
    return plan(tokens, cotangent, blocks_w, lowrank_u, lowrank_v)


def solution(mesh):
    in_specs = (
        P("dp", "mp"),
        P("dp", "mp"),
        P("mp", None, None, None),
        P("mp", None),
        P(None, "mp"),
    )
    out_specs = (
        P("dp", "mp"),
        P("dp", "mp", None, None),
        P(("mp", "dp"), None),
        P(None, ("mp", "dp")),
    )
    return jax.shard_map(
        per_device, mesh=mesh, in_specs=in_specs, out_specs=out_specs, check_vma=False
    )
```

```python
import math

import jax
import jax.numpy as jnp
from jax import lax
from jax.experimental import pallas as pl
from jax.experimental.pallas import tpu as pltpu
from jax.sharding import PartitionSpec as P

F32 = jnp.float32
BF16 = jnp.bfloat16
ROOM = 56 * 1024 * 1024
QUICK = pl.CostEstimate(flops=0, bytes_accessed=0, transcendentals=0)
GATHER = (2, 1)
REDUCE = (1, 2)


def swap(value, axis, apart):
    count = lax.axis_size(axis)
    return lax.ppermute(value, axis, [(i, i ^ apart) for i in range(count)])


def tie(values, *others):
    return lax.optimization_barrier((values, others))[0]


def dot(a, b, dims):
    return lax.dot_general(a, b, (dims, ((), ())), preferred_element_type=F32)


def ordered(mine, theirs, bit, axis):
    return jnp.where(
        bit == 0,
        jnp.concatenate([mine, theirs], axis),
        jnp.concatenate([theirs, mine], axis),
    )


def call(body, **kwargs):
    return pl.pallas_call(
        body,
        compiler_params=pltpu.CompilerParams(vmem_limit_bytes=ROOM),
        cost_estimate=QUICK,
        **kwargs,
    )


def prefetched(body, me, grid, in_specs, out_specs, out_shape, operands, **kwargs):
    spec = pltpu.PrefetchScalarGridSpec(
        num_scalar_prefetch=1, grid=grid, in_specs=in_specs, out_specs=out_specs
    )
    return call(body, grid_spec=spec, out_shape=out_shape, **kwargs)(me, *operands)


def partner_term(cot, weights, slot):
    blocks, _, width = weights.shape[:3]
    rows = cot.shape[0]

    def body(c, w, o):
        o[...] = dot(c[...], w[0, 0], ((1,), (1,))).astype(BF16)

    return call(
        body,
        grid=(blocks,),
        in_specs=[
            pl.BlockSpec((rows, width), lambda j: (0, j)),
            pl.BlockSpec((1, 1, width, width), lambda j: (j, slot, 0, 0)),
        ],
        out_specs=pl.BlockSpec((rows, width), lambda j: (0, j)),
        out_shape=jax.ShapeDtypeStruct((rows, blocks * width), BF16),
    )(cot, weights)


def own_terms(cot, weights, count):
    blocks, _, width = weights.shape[:3]
    rows = cot.shape[0]
    tile = width // 2
    tiles = width // tile

    def body(c, *refs):
        o = refs[-1]
        for block in range(blocks):

            @pl.when(pl.program_id(0) == block)
            def _():
                value = None
                for s in range(count):
                    other = block ^ ((1 << s) >> 1)
                    more = dot(c[:, other * width : (other + 1) * width], refs[s][0, 0], ((1,), (1,)))
                    value = more if value is None else value + more
                o[...] = value

    def weight(s):
        return pl.BlockSpec((1, 1, tile, width), lambda i, t: (i ^ ((1 << s) >> 1), s, t, 0))

    return call(
        body,
        grid=(blocks, tiles),
        in_specs=[pl.BlockSpec((rows, blocks * width), lambda i, t: (0, 0))]
        + [weight(s) for s in range(count)],
        out_specs=pl.BlockSpec((rows, tile), lambda i, t: (0, i * tiles + t)),
        out_shape=jax.ShapeDtypeStruct((rows, blocks * width), F32),
    )(cot, *[weights] * count)


def projections(core, tokens, cot, u, v):
    rows, width = tokens.shape
    rank = u.shape[1]
    tile = rows // 2

    def body(core_ref, t, c, u_ref, v_ref, kept, sent):
        low = dot(t[...], u_ref[...], ((1,), (0,)))
        back = dot(c[...], v_ref[...], ((1,), (1,)))
        first = core_ref[0] == 0
        kept[...] = jnp.where(first, low, back)
        sent[...] = jnp.where(first, back, low)

    shape = jax.ShapeDtypeStruct((rows, rank), F32)
    return call(
        body,
        grid=(rows // tile,),
        in_specs=[
            pl.BlockSpec(memory_space=pltpu.SMEM),
            pl.BlockSpec((tile, width), lambda r: (r, 0)),
            pl.BlockSpec((tile, width), lambda r: (r, 0)),
            pl.BlockSpec((width, rank), lambda r: (0, 0)),
            pl.BlockSpec((rank, width), lambda r: (0, 0)),
        ],
        out_specs=[pl.BlockSpec((tile, rank), lambda r: (r, 0))] * 2,
        out_shape=[shape, shape],
    )(core, tokens, cot, u, v)


def pieces(me, tokens, cot, blocks, part):
    rows, width = tokens.shape
    width //= blocks
    tile = rows // 4

    def body(me_ref, t, c, held, *given):
        def shard(block, x):
            start = pl.multiple_of(block * width + (me_ref[0] ^ x) * part, part)
            return t[:, pl.ds(start, part)]

        for j in range(blocks):
            held[:, 2 * j * part : (2 * j + 1) * part] = shard(j, 0)
            held[:, (2 * j + 1) * part : (2 * j + 2) * part] = shard(j, REDUCE[j])
            for at, block in enumerate((j, j ^ 1)):
                start = 2 * at * part
                given[j][:, start : start + part] = shard(block, GATHER[j])
                given[j][:, start + part : start + 2 * part] = shard(block, GATHER[j] ^ REDUCE[j])
            given[j][:, 4 * part :] = c[:, j * width : (j + 1) * width]

    widths = [2 * blocks * part] + [4 * part + width] * blocks
    return prefetched(
        body,
        me,
        (rows // tile,),
        [pl.BlockSpec((tile, blocks * width), lambda r, m: (r, 0))] * 2,
        [pl.BlockSpec((tile, w), lambda r, m: (r, 0)) for w in widths],
        [jax.ShapeDtypeStruct((rows, w), BF16) for w in widths],
        (tokens, cot),
    )


def slot_sums(me, j, tokens, cot, given, local, partners, part):
    rows = tokens.shape[0]
    width = given.shape[1] - 4 * part
    shards = width // part
    slots = 2 * local + len(partners)
    tile = width // 2
    mine = 4 * local

    def body(me_ref, *refs):
        far = refs[mine + 2 * local : -4]
        c0, c1, kept, sent = refs[-4:]
        first = list(refs[:mine]) + list(far[0::2])
        second = list(refs[mine : mine + 2 * local]) + list(far[1::2])
        value = dot(jnp.concatenate([r[...] for r in first], 1), c0[...], ((0,), (0,)))
        value = value + dot(jnp.concatenate([r[...] for r in second], 1), c1[...], ((0,), (0,)))
        for s in range(slots):
            kept[s] = value[2 * s * part : (2 * s + 1) * part]
            sent[s] = value[(2 * s + 1) * part : (2 * s + 2) * part].astype(BF16)

    def shard(block, x):
        return pl.BlockSpec((rows, part), lambda t, m: (0, block * shards + (m[0] ^ x)))

    def pair(at):
        return pl.BlockSpec((rows, 2 * part), lambda t, m: (0, at))

    in_specs, operands = [], []
    if local:
        in_specs += [shard(j, 0), shard(j, REDUCE[j]), shard(j ^ 1, 0), shard(j ^ 1, REDUCE[j])]
        in_specs += [pair(0), pair(1)]
        operands += [tokens] * 4 + [given] * 2
    for one, two in partners:
        in_specs += [pair(one[1]), pair(two[1])]
        operands += [one[0], two[0]]
    in_specs += [
        pl.BlockSpec((rows, tile), lambda t, m: (0, j * (width // tile) + t)),
        pl.BlockSpec((rows, tile), lambda t, m: (0, 4 * part // tile + t)),
    ]
    out = pl.BlockSpec((slots, part, tile), lambda t, m: (0, 0, t))
    shape = (slots, part, width)
    return prefetched(
        body,
        me,
        (width // tile,),
        in_specs,
        [out, out],
        [jax.ShapeDtypeStruct(shape, F32), jax.ShapeDtypeStruct(shape, BF16)],
        (*operands, cot, given),
    )


def all_grads(kept, got, scale):
    blocks = len(kept)
    counts = [k.shape[0] for k in kept[0]]
    _, part, width = kept[0][0].shape
    slots = sum(counts)
    tile = width // 4

    def body(*refs):
        o = refs[-1]
        refs = iter(refs)
        for j in range(blocks):
            at = 0
            for count in counts:
                mine, theirs = next(refs), next(refs)
                for s in range(count):
                    o[:, at + s, j, :] = (mine[s] + theirs[s].astype(F32)) * scale
                at += count

    operands = [
        x for j in range(blocks) for pair in zip(kept[j], got[j]) for x in pair
    ]
    out = call(
        body,
        grid=(width // tile,),
        in_specs=[pl.BlockSpec((x.shape[0], part, tile), lambda t: (0, 0, t)) for x in operands],
        out_specs=pl.BlockSpec((part, slots, blocks, tile), lambda t: (0, 0, 0, t)),
        out_shape=jax.ShapeDtypeStruct((part, slots, blocks, width), F32),
    )(*operands)
    return jnp.transpose(out, (0, 2, 1, 3))


def gathered(given, width):
    rows = given[0].shape[0]

    def body(*refs):
        for j in range(len(given)):

            @pl.when(pl.program_id(0) == j)
            def _():
                refs[-1][...] = refs[j][...]

    return call(
        body,
        grid=(len(given),),
        in_specs=[pl.BlockSpec((rows, width), lambda j: (0, 0)) for _ in given],
        out_specs=pl.BlockSpec((rows, width), lambda j: (0, j)),
        out_shape=jax.ShapeDtypeStruct((rows, len(given) * width), BF16),
    )(*given)


def joined(base, near, low_back, u):
    rows, width = base.shape
    tile = width // 4
    skipped = (near.shape[1] - width) // tile

    def body(b, n, l, u_ref, o):
        o[...] = b[...] + n[...].astype(F32) + dot(l[...], u_ref[...], ((1,), (1,)))

    block = pl.BlockSpec((rows, tile), lambda t: (0, t))
    return call(
        body,
        grid=(width // tile,),
        in_specs=[
            block,
            pl.BlockSpec((rows, tile), lambda t: (0, skipped + t)),
            pl.BlockSpec(low_back.shape, lambda t: (0, 0)),
            pl.BlockSpec((tile, u.shape[1]), lambda t: (t, 0)),
        ],
        out_specs=block,
        out_shape=jax.ShapeDtypeStruct(base.shape, F32),
    )(base, near, low_back, u)


def summed_rows(term):
    me = lax.axis_index("dp")
    size = term.shape[0] // 4
    parts = [lax.dynamic_slice_in_dim(term, (me ^ x) * size, size, 0) for x in range(4)]
    got = swap(jnp.concatenate([parts[1], parts[3]], 0).astype(BF16), "dp", 1).astype(F32)
    mine, theirs = parts[0] + got[:size], parts[2] + got[size:]
    return mine + swap(theirs.astype(BF16), "dp", 2).astype(F32)


def square(tokens, cotangent, blocks_w, lowrank_u, lowrank_v):
    lb, slots, bw = blocks_w.shape[:3]
    rows = tokens.shape[0]
    n_dp = lax.axis_size("dp")
    part = bw // n_dp
    scale = 1.0 / math.sqrt(rows * n_dp)
    me = jnp.reshape(lax.axis_index("dp"), (1,)).astype(jnp.int32)
    mp_me = lax.axis_index("mp")
    core, side = mp_me & 1, mp_me >> 1 & 1
    half = rows // 2
    near, far = 2, (3, 4)
    apart = {s: (1 << (s - 1)) // lb for s in (near, *far)}

    held, *given = pieces(me, tokens, cotangent, lb, part)
    given = [swap(g, "dp", GATHER[j]) for j, g in enumerate(given)]
    held_in = {s: swap(held, "mp", apart[s]) for s in far}

    tokens1, cot1 = tie((tokens, cotangent), held)
    kept, sent = projections(
        jnp.reshape(core, (1,)).astype(jnp.int32), tokens1, cot1, lowrank_u, lowrank_v
    )
    got = swap(sent, "mp", 1)
    cot1 = tie(cot1, kept)
    out = {near: partner_term(cot1, blocks_w, near)}
    kept = kept + tie(got, out)
    for s in far:
        cot1 = tie(cot1, out)
        out[s] = partner_term(cot1, blocks_w, s)
    base = own_terms(tie(cot1, out), blocks_w, 2)
    kept = tie(kept, base)
    sent = lax.dynamic_slice_in_dim(kept, (1 - side) * half, half, 0)
    kept = lax.dynamic_slice_in_dim(kept, side * half, half, 0)
    got = swap(sent, "mp", 2)

    near_out = jnp.concatenate([held, out[near]], 1)
    given, held_in, out, near_out, got = tie((given, held_in, out, near_out, got), base)
    more = gathered(given, 2 * part)
    more_in = {s: swap(more, "mp", apart[s]) for s in far}
    near_in = swap(near_out, "mp", apart[near])
    near_more = swap(more, "mp", apart[near])
    kept = kept + got
    got = swap(kept, "mp", 4)

    kept = (kept + got).astype(BF16)
    got = swap(kept, "mp", 2)
    whole = ordered(kept, got, side, 0)
    other = swap(whole, "mp", 1)
    low_in = jnp.where(core == 0, whole, other)
    low_back = jnp.where(core == 0, other, whole)

    out = tie(out, near_more, near_in)
    more_in[3], last = tie((more_in[3], out[3]))
    far_in = [swap(last, "mp", apart[3]), swap(out[4], "mp", apart[4])]

    sums, tokens1 = [], tokens
    for j in range(lb):
        partners = [(near_in, near_more)] + [(held_in[s], more_in[s]) for s in far]
        partners = [((one, j), (two, j)) for one, two in partners]
        sums.append(slot_sums(me, j, tokens1, cotangent, given[j], True, partners, part))
        tokens1 = tie(tokens1, sums[j])
    sums_in = [swap(sums[j][1], "dp", REDUCE[j]) for j in range(lb)]

    u_term = dot(tokens, low_back, ((0,), (0,)))
    v_term = dot(cotangent, low_in, ((0,), (0,)))
    uv = summed_rows(jnp.concatenate([u_term, v_term], 1)) * scale
    rank = lowrank_u.shape[1]
    grad_u, grad_v = uv[:, :rank], uv[:, rank:].T
    full = joined(base, near_in, low_back, lowrank_u)
    sums_in = tie(sums_in, full)
    grad_blocks = all_grads([[s[0]] for s in sums], [[s] for s in sums_in], scale)
    far_in, full = tie((far_in, full), grad_blocks)
    grad_tokens = full + far_in[0].astype(F32) + far_in[1].astype(F32)
    return (grad_tokens, grad_blocks, grad_u, grad_v)


def general(tokens, cotangent, blocks_w, lowrank_u, lowrank_v):
    lb, slots, bw = blocks_w.shape[:3]
    rows = tokens.shape[0]
    n_dp = lax.axis_size("dp")
    part = bw // n_dp
    scale = 1.0 / math.sqrt(rows * n_dp)

    def blocks_of(value):
        return value.reshape(value.shape[0], lb, -1)

    def partner(value, slot):
        distance = (1 << slot) >> 1
        if distance < lb:
            return jnp.stack([value[:, j ^ distance] for j in range(lb)], 1)
        return swap(value, "mp", distance // lb)

    low = dot(tokens, lowrank_u, ((1,), (0,)))
    back = dot(cotangent, lowrank_v, ((1,), (1,)))
    low, back = lax.psum((low, back), "mp")
    low, back = low.astype(BF16), back.astype(BF16)

    turned = tokens.reshape(rows, lb, n_dp, part)
    turned = lax.all_to_all(turned, "dp", 2, 0, tiled=True).reshape(n_dp * rows, lb, part)
    cot_all = blocks_of(lax.all_gather(cotangent, "dp", tiled=True))
    cot = blocks_of(cotangent)
    total = blocks_of(dot(back, lowrank_u, ((1,), (1,))))
    grads = []
    for s in range(slots):
        term = jnp.einsum("tbo,bio->tbi", cot, blocks_w[:, s], preferred_element_type=F32)
        if (1 << s) >> 1 >= lb:
            term = term.astype(BF16)
        total = total + partner(term, s).astype(F32)
        grads.append(
            jnp.einsum("tbi,tbo->ibo", partner(turned, s), cot_all, preferred_element_type=F32)
        )
    grad_blocks = jnp.stack(grads, 2) * scale
    u_term = dot(tokens, back, ((0,), (0,)))
    v_term = dot(low, cotangent, ((0,), (0,)))
    grad_u = lax.psum_scatter(u_term, "dp", scatter_dimension=0, tiled=True)
    grad_v = lax.psum_scatter(v_term, "dp", scatter_dimension=1, tiled=True)
    return (total.reshape(rows, lb * bw), grad_blocks, grad_u * scale, grad_v * scale)


def per_device(tokens, cotangent, blocks_w, lowrank_u, lowrank_v):
    sizes = (blocks_w.shape[0], lax.axis_size("dp"), lax.axis_size("mp"))
    plan = square if sizes == (2, 4, 8) and blocks_w.shape[1] == 5 else general
    return plan(tokens, cotangent, blocks_w, lowrank_u, lowrank_v)


def solution(mesh):
    in_specs = (
        P("dp", "mp"),
        P("dp", "mp"),
        P("mp", None, None, None),
        P("mp", None),
        P(None, "mp"),
    )
    out_specs = (
        P("dp", "mp"),
        P("dp", "mp", None, None),
        P(("mp", "dp"), None),
        P(None, ("mp", "dp")),
    )
    return jax.shard_map(
        per_device, mesh=mesh, in_specs=in_specs, out_specs=out_specs, check_vma=False
    )
```

```python
import math

import jax
import jax.numpy as jnp
from jax import lax
from jax.experimental import pallas as pl
from jax.experimental.pallas import tpu as pltpu
from jax.sharding import PartitionSpec as P

F32 = jnp.float32
BF16 = jnp.bfloat16
ROOM = 56 * 1024 * 1024
QUICK = pl.CostEstimate(flops=0, bytes_accessed=0, transcendentals=0)
GATHER = (2, 1)
REDUCE = (1, 2)


def swap(value, axis, apart):
    count = lax.axis_size(axis)
    return lax.ppermute(value, axis, [(i, i ^ apart) for i in range(count)])


def tie(values, *others):
    return lax.optimization_barrier((values, others))[0]


def dot(a, b, dims):
    return lax.dot_general(a, b, (dims, ((), ())), preferred_element_type=F32)


def ordered(mine, theirs, bit, axis):
    return jnp.where(
        bit == 0,
        jnp.concatenate([mine, theirs], axis),
        jnp.concatenate([theirs, mine], axis),
    )


def call(body, **kwargs):
    return pl.pallas_call(
        body,
        compiler_params=pltpu.CompilerParams(vmem_limit_bytes=ROOM),
        cost_estimate=QUICK,
        **kwargs,
    )


def prefetched(body, me, grid, in_specs, out_specs, out_shape, operands, **kwargs):
    spec = pltpu.PrefetchScalarGridSpec(
        num_scalar_prefetch=1, grid=grid, in_specs=in_specs, out_specs=out_specs
    )
    return call(body, grid_spec=spec, out_shape=out_shape, **kwargs)(me, *operands)


def partner_term(cot, weights, slot, cut=0):
    blocks, _, width = weights.shape[:3]
    rows = cot.shape[0]
    heights = (cut, rows - cut) if cut else (rows,)

    def body(c, w, *out):
        value = dot(c[...], w[0, 0], ((1,), (1,))).astype(BF16)
        at = 0
        for o in out:
            o[...] = value[at : at + o.shape[0]]
            at += o.shape[0]

    parts = call(
        body,
        grid=(blocks,),
        in_specs=[
            pl.BlockSpec((rows, width), lambda j: (0, j)),
            pl.BlockSpec((1, 1, width, width), lambda j: (j, slot, 0, 0)),
        ],
        out_specs=[pl.BlockSpec((h, width), lambda j: (0, j)) for h in heights],
        out_shape=[jax.ShapeDtypeStruct((h, blocks * width), BF16) for h in heights],
    )(cot, weights)
    return parts if cut else parts[0]


def own_terms(cot, weights, count):
    blocks, _, width = weights.shape[:3]
    rows = cot.shape[0]
    tile = width // 2
    tiles = width // tile

    def body(c, *refs):
        o = refs[-1]
        for block in range(blocks):

            @pl.when(pl.program_id(0) == block)
            def _():
                value = None
                for s in range(count):
                    other = block ^ ((1 << s) >> 1)
                    more = dot(c[:, other * width : (other + 1) * width], refs[s][0, 0], ((1,), (1,)))
                    value = more if value is None else value + more
                o[...] = value

    def weight(s):
        return pl.BlockSpec((1, 1, tile, width), lambda i, t: (i ^ ((1 << s) >> 1), s, t, 0))

    return call(
        body,
        grid=(blocks, tiles),
        in_specs=[pl.BlockSpec((rows, blocks * width), lambda i, t: (0, 0))]
        + [weight(s) for s in range(count)],
        out_specs=pl.BlockSpec((rows, tile), lambda i, t: (0, i * tiles + t)),
        out_shape=jax.ShapeDtypeStruct((rows, blocks * width), F32),
    )(cot, *[weights] * count)


def projections(core, tokens, cot, u, v):
    rows, width = tokens.shape
    rank = u.shape[1]
    tile = rows // 2

    def body(core_ref, t, c, u_ref, v_ref, kept, sent):
        low = dot(t[...], u_ref[...], ((1,), (0,)))
        back = dot(c[...], v_ref[...], ((1,), (1,)))
        first = core_ref[0] == 0
        kept[...] = jnp.where(first, low, back)
        sent[...] = jnp.where(first, back, low)

    shape = jax.ShapeDtypeStruct((rows, rank), F32)
    return call(
        body,
        grid=(rows // tile,),
        in_specs=[
            pl.BlockSpec(memory_space=pltpu.SMEM),
            pl.BlockSpec((tile, width), lambda r: (r, 0)),
            pl.BlockSpec((tile, width), lambda r: (r, 0)),
            pl.BlockSpec((width, rank), lambda r: (0, 0)),
            pl.BlockSpec((rank, width), lambda r: (0, 0)),
        ],
        out_specs=[pl.BlockSpec((tile, rank), lambda r: (r, 0))] * 2,
        out_shape=[shape, shape],
    )(core, tokens, cot, u, v)


def pieces(me, tokens, cot, blocks, part):
    rows, width = tokens.shape
    width //= blocks
    tile = rows // 2

    def body(me_ref, t, c, held, *given):
        def shard(block, x):
            start = pl.multiple_of(block * width + (me_ref[0] ^ x) * part, part)
            return t[:, pl.ds(start, part)]

        for j in range(blocks):
            held[:, 2 * j * part : (2 * j + 1) * part] = shard(j, 0)
            held[:, (2 * j + 1) * part : (2 * j + 2) * part] = shard(j, REDUCE[j])
            for at, block in enumerate((j, j ^ 1)):
                start = 2 * at * part
                given[j][:, start : start + part] = shard(block, GATHER[j])
                given[j][:, start + part : start + 2 * part] = shard(block, GATHER[j] ^ REDUCE[j])
            given[j][:, 4 * part :] = c[:, j * width : (j + 1) * width]

    widths = [2 * blocks * part] + [4 * part + width] * blocks
    return prefetched(
        body,
        me,
        (rows // tile,),
        [pl.BlockSpec((tile, blocks * width), lambda r, m: (r, 0))] * 2,
        [pl.BlockSpec((tile, w), lambda r, m: (r, 0)) for w in widths],
        [jax.ShapeDtypeStruct((rows, w), BF16) for w in widths],
        (tokens, cot),
    )


def slot_sums(me, j, tokens, cot, given, local, partners, part):
    rows = tokens.shape[0]
    width = given.shape[1] - 4 * part
    shards = width // part
    slots = 2 * local + len(partners)
    tile = width // 2
    mine = 4 * local

    def body(me_ref, *refs):
        far = refs[mine + 2 * local : -4]
        c0, c1, kept, sent = refs[-4:]
        first = list(refs[:mine]) + list(far[0::2])
        second = list(refs[mine : mine + 2 * local]) + list(far[1::2])
        value = dot(jnp.concatenate([r[...] for r in first], 1), c0[...], ((0,), (0,)))
        value = value + dot(jnp.concatenate([r[...] for r in second], 1), c1[...], ((0,), (0,)))
        for s in range(slots):
            kept[s] = value[2 * s * part : (2 * s + 1) * part]
            sent[s] = value[(2 * s + 1) * part : (2 * s + 2) * part].astype(BF16)

    def shard(block, x):
        return pl.BlockSpec((rows, part), lambda t, m: (0, block * shards + (m[0] ^ x)))

    def pair(at):
        return pl.BlockSpec((rows, 2 * part), lambda t, m: (0, at))

    in_specs, operands = [], []
    if local:
        in_specs += [shard(j, 0), shard(j, REDUCE[j]), shard(j ^ 1, 0), shard(j ^ 1, REDUCE[j])]
        in_specs += [pair(0), pair(1)]
        operands += [tokens] * 4 + [given] * 2
    for one, two in partners:
        in_specs += [pair(one[1]), pair(two[1])]
        operands += [one[0], two[0]]
    in_specs += [
        pl.BlockSpec((rows, tile), lambda t, m: (0, j * (width // tile) + t)),
        pl.BlockSpec((rows, tile), lambda t, m: (0, 4 * part // tile + t)),
    ]
    out = pl.BlockSpec((slots, part, tile), lambda t, m: (0, 0, t))
    shape = (slots, part, width)
    return prefetched(
        body,
        me,
        (width // tile,),
        in_specs,
        [out, out],
        [jax.ShapeDtypeStruct(shape, F32), jax.ShapeDtypeStruct(shape, BF16)],
        (*operands, cot, given),
    )


def all_grads(kept, got, scale):
    blocks = len(kept)
    counts = [k.shape[0] for k in kept[0]]
    _, part, width = kept[0][0].shape
    slots = sum(counts)
    tile = width // 4

    def body(*refs):
        o = refs[-1]
        refs = iter(refs)
        for j in range(blocks):
            at = 0
            for count in counts:
                mine, theirs = next(refs), next(refs)
                for s in range(count):
                    o[:, at + s, j, :] = (mine[s] + theirs[s].astype(F32)) * scale
                at += count

    operands = [
        x for j in range(blocks) for pair in zip(kept[j], got[j]) for x in pair
    ]
    out = call(
        body,
        grid=(width // tile,),
        in_specs=[pl.BlockSpec((x.shape[0], part, tile), lambda t: (0, 0, t)) for x in operands],
        out_specs=pl.BlockSpec((part, slots, blocks, tile), lambda t: (0, 0, 0, t)),
        out_shape=jax.ShapeDtypeStruct((part, slots, blocks, width), F32),
    )(*operands)
    return jnp.transpose(out, (0, 2, 1, 3))


def gathered(given, width):
    rows = given[0].shape[0]

    def body(*refs):
        for j in range(len(given)):

            @pl.when(pl.program_id(0) == j)
            def _():
                refs[-1][...] = refs[j][...]

    return call(
        body,
        grid=(len(given),),
        in_specs=[pl.BlockSpec((rows, width), lambda j: (0, 0)) for _ in given],
        out_specs=pl.BlockSpec((rows, width), lambda j: (0, j)),
        out_shape=jax.ShapeDtypeStruct((rows, len(given) * width), BF16),
    )(*given)


def joined(base, near, low_back, u):
    rows, width = base.shape
    tile = width // 4
    skipped = (near.shape[1] - width) // tile

    def body(b, n, l, u_ref, o):
        o[...] = b[...] + n[...].astype(F32) + dot(l[...], u_ref[...], ((1,), (1,)))

    block = pl.BlockSpec((rows, tile), lambda t: (0, t))
    return call(
        body,
        grid=(width // tile,),
        in_specs=[
            block,
            pl.BlockSpec((rows, tile), lambda t: (0, skipped + t)),
            pl.BlockSpec(low_back.shape, lambda t: (0, 0)),
            pl.BlockSpec((tile, u.shape[1]), lambda t: (t, 0)),
        ],
        out_specs=block,
        out_shape=jax.ShapeDtypeStruct(base.shape, F32),
    )(base, near, low_back, u)


def added(base, terms, first):
    rows, width = terms[0].shape
    tile = rows // 4 if rows > 256 else rows

    def body(b, *refs):
        value = b[...]
        for ref in refs[:-1]:
            value = value + ref[...].astype(F32)
        refs[-1][...] = value

    block = pl.BlockSpec((tile, width), lambda r: (r + first // tile, 0))
    return call(
        body,
        grid=(rows // tile,),
        in_specs=[block] + [pl.BlockSpec((tile, width), lambda r: (r, 0)) for _ in terms],
        out_specs=block,
        out_shape=jax.ShapeDtypeStruct(base.shape, F32),
        input_output_aliases={0: 0},
    )(base, *terms)


def summed_rows(term, before):
    me = lax.axis_index("dp")
    size = term.shape[0] // 4
    parts = [lax.dynamic_slice_in_dim(term, (me ^ x) * size, size, 0) for x in range(4)]
    got = swap(jnp.concatenate([parts[1], parts[3]], 0).astype(BF16), "dp", 1)
    got = tie(got, before[0]).astype(F32)
    mine, theirs = parts[0] + got[:size], parts[2] + got[size:]
    got = swap(theirs.astype(BF16), "dp", 2)
    return mine + tie(got, before[1]).astype(F32)


def square(tokens, cotangent, blocks_w, lowrank_u, lowrank_v):
    lb, slots, bw = blocks_w.shape[:3]
    rows = tokens.shape[0]
    n_dp = lax.axis_size("dp")
    part = bw // n_dp
    scale = 1.0 / math.sqrt(rows * n_dp)
    me = jnp.reshape(lax.axis_index("dp"), (1,)).astype(jnp.int32)
    mp_me = lax.axis_index("mp")
    core, side = mp_me & 1, mp_me >> 1 & 1
    half, cut = rows // 2, rows // 12 * 11
    near, far = 2, (3, 4)
    apart = {s: (1 << (s - 1)) // lb for s in (near, *far)}

    held, *given = pieces(me, tokens, cotangent, lb, part)
    given = [swap(g, "dp", GATHER[j]) for j, g in enumerate(given)]
    held_in = {s: swap(held, "mp", apart[s]) for s in far}

    tokens1, cot1 = tie((tokens, cotangent), held)
    kept, sent = projections(
        jnp.reshape(core, (1,)).astype(jnp.int32), tokens1, cot1, lowrank_u, lowrank_v
    )
    got = swap(sent, "mp", 1)
    cot1 = tie(cot1, kept)
    out = {near: partner_term(cot1, blocks_w, near)}
    kept = kept + tie(got, out)
    for s in far:
        cot1 = tie(cot1, out)
        out[s] = partner_term(cot1, blocks_w, s, cut)
    base = own_terms(tie(cot1, out), blocks_w, 2)
    kept = tie(kept, base)
    sent = lax.dynamic_slice_in_dim(kept, (1 - side) * half, half, 0)
    kept = lax.dynamic_slice_in_dim(kept, side * half, half, 0)
    got = swap(sent, "mp", 2)

    near_out = jnp.concatenate([held, out[near]], 1)
    given = tie(given, base)
    more = gathered(given, 2 * part)
    given, held_in, out, near_out, got, more = tie((given, held_in, out, near_out, got, more))
    more_in = {3: swap(more, "mp", apart[3])}
    near_in = swap(near_out, "mp", apart[near])
    near_more = swap(more, "mp", apart[near])
    kept = kept + got
    got = swap(kept, "mp", 4)
    got, more4 = tie((got, more))
    more_in[4] = swap(more4, "mp", apart[4])

    kept = (kept + got).astype(BF16)
    got = swap(kept, "mp", 2)
    got, near_in, near_more = tie((got, near_in, near_more))
    whole = ordered(kept, got, side, 0)
    other = swap(whole, "mp", 1)
    low_in = jnp.where(core == 0, whole, other)
    low_back = jnp.where(core == 0, other, whole)

    out = tie(out, near_more, near_in)
    more_in[3], first = tie((more_in[3], out[3][0]))
    far_in = [swap(first, "mp", apart[3]), swap(out[4][0], "mp", apart[4])]

    sums, tokens1 = [], tokens
    for j in range(lb):
        partners = [(near_in, near_more)] + [(held_in[s], more_in[s]) for s in far]
        partners = [((one, j), (two, j)) for one, two in partners]
        sums.append(slot_sums(me, j, tokens1, cotangent, given[j], True, partners, part))
    sums_in = [swap(sums[j][1], "dp", REDUCE[j]) for j in range(lb)]

    full = joined(base, near_in, low_back, lowrank_u)
    sums_in = tie(sums_in, full)
    grad_blocks = all_grads([[s[0]] for s in sums], [[s] for s in sums_in], scale)

    u_term = dot(tokens, low_back, ((0,), (0,)))
    v_term = dot(cotangent, low_in, ((0,), (0,)))
    uv = summed_rows(jnp.concatenate([u_term, v_term], 1), (full, grad_blocks)) * scale
    rank = lowrank_u.shape[1]
    grad_u, grad_v = uv[:, :rank], uv[:, rank:].T
    last_in = [swap(out[s][1], "mp", apart[s]) for s in far]
    far_in, full = tie((far_in, full), grad_blocks)
    full = added(full, far_in, 0)
    last_in = tie(last_in, full)
    grad_tokens = added(full, last_in, cut)
    return (grad_tokens, grad_blocks, grad_u, grad_v)


def general(tokens, cotangent, blocks_w, lowrank_u, lowrank_v):
    lb, slots, bw = blocks_w.shape[:3]
    rows = tokens.shape[0]
    n_dp = lax.axis_size("dp")
    part = bw // n_dp
    scale = 1.0 / math.sqrt(rows * n_dp)

    def blocks_of(value):
        return value.reshape(value.shape[0], lb, -1)

    def partner(value, slot):
        distance = (1 << slot) >> 1
        if distance < lb:
            return jnp.stack([value[:, j ^ distance] for j in range(lb)], 1)
        return swap(value, "mp", distance // lb)

    low = dot(tokens, lowrank_u, ((1,), (0,)))
    back = dot(cotangent, lowrank_v, ((1,), (1,)))
    low, back = lax.psum((low, back), "mp")
    low, back = low.astype(BF16), back.astype(BF16)

    turned = tokens.reshape(rows, lb, n_dp, part)
    turned = lax.all_to_all(turned, "dp", 2, 0, tiled=True).reshape(n_dp * rows, lb, part)
    cot_all = blocks_of(lax.all_gather(cotangent, "dp", tiled=True))
    cot = blocks_of(cotangent)
    total = blocks_of(dot(back, lowrank_u, ((1,), (1,))))
    grads = []
    for s in range(slots):
        term = jnp.einsum("tbo,bio->tbi", cot, blocks_w[:, s], preferred_element_type=F32)
        if (1 << s) >> 1 >= lb:
            term = term.astype(BF16)
        total = total + partner(term, s).astype(F32)
        grads.append(
            jnp.einsum("tbi,tbo->ibo", partner(turned, s), cot_all, preferred_element_type=F32)
        )
    grad_blocks = jnp.stack(grads, 2) * scale
    u_term = dot(tokens, back, ((0,), (0,)))
    v_term = dot(low, cotangent, ((0,), (0,)))
    grad_u = lax.psum_scatter(u_term, "dp", scatter_dimension=0, tiled=True)
    grad_v = lax.psum_scatter(v_term, "dp", scatter_dimension=1, tiled=True)
    return (total.reshape(rows, lb * bw), grad_blocks, grad_u * scale, grad_v * scale)


def per_device(tokens, cotangent, blocks_w, lowrank_u, lowrank_v):
    sizes = (blocks_w.shape[0], lax.axis_size("dp"), lax.axis_size("mp"))
    plan = square if sizes == (2, 4, 8) and blocks_w.shape[1] == 5 else general
    return plan(tokens, cotangent, blocks_w, lowrank_u, lowrank_v)


def solution(mesh):
    in_specs = (
        P("dp", "mp"),
        P("dp", "mp"),
        P("mp", None, None, None),
        P("mp", None),
        P(None, "mp"),
    )
    out_specs = (
        P("dp", "mp"),
        P("dp", "mp", None, None),
        P(("mp", "dp"), None),
        P(None, ("mp", "dp")),
    )
    return jax.shard_map(
        per_device, mesh=mesh, in_specs=in_specs, out_specs=out_specs, check_vma=False
    )
```

```python
import math

import jax
import jax.numpy as jnp
from jax import lax
from jax.experimental import pallas as pl
from jax.experimental.pallas import tpu as pltpu
from jax.sharding import PartitionSpec as P

F32 = jnp.float32
BF16 = jnp.bfloat16
ROOM = 56 * 1024 * 1024
QUICK = pl.CostEstimate(flops=0, bytes_accessed=0, transcendentals=0)
GATHER = (2, 1)
REDUCE = (1, 2)


def swap(value, axis, apart):
    count = lax.axis_size(axis)
    return lax.ppermute(value, axis, [(i, i ^ apart) for i in range(count)])


def tie(values, *others):
    return lax.optimization_barrier((values, others))[0]


def dot(a, b, dims):
    return lax.dot_general(a, b, (dims, ((), ())), preferred_element_type=F32)


def ordered(mine, theirs, bit, axis):
    return jnp.where(
        bit == 0,
        jnp.concatenate([mine, theirs], axis),
        jnp.concatenate([theirs, mine], axis),
    )


def call(body, **kwargs):
    return pl.pallas_call(
        body,
        compiler_params=pltpu.CompilerParams(vmem_limit_bytes=ROOM),
        cost_estimate=QUICK,
        **kwargs,
    )


def prefetched(body, me, grid, in_specs, out_specs, out_shape, operands, **kwargs):
    spec = pltpu.PrefetchScalarGridSpec(
        num_scalar_prefetch=1, grid=grid, in_specs=in_specs, out_specs=out_specs
    )
    return call(body, grid_spec=spec, out_shape=out_shape, **kwargs)(me, *operands)


def partner_term(cot, weights, slot, cut=0):
    blocks, _, width = weights.shape[:3]
    rows = cot.shape[0]
    heights = (cut, rows - cut) if cut else (rows,)

    def body(c, w, *out):
        value = dot(c[...], w[0, 0], ((1,), (1,))).astype(BF16)
        at = 0
        for o in out:
            o[...] = value[at : at + o.shape[0]]
            at += o.shape[0]

    parts = call(
        body,
        grid=(blocks,),
        in_specs=[
            pl.BlockSpec((rows, width), lambda j: (0, j)),
            pl.BlockSpec((1, 1, width, width), lambda j: (j, slot, 0, 0)),
        ],
        out_specs=[pl.BlockSpec((h, width), lambda j: (0, j)) for h in heights],
        out_shape=[jax.ShapeDtypeStruct((h, blocks * width), BF16) for h in heights],
    )(cot, weights)
    return parts if cut else parts[0]


def own_terms(cot, weights, count):
    blocks, _, width = weights.shape[:3]
    rows = cot.shape[0]
    tile = width // 2
    tiles = width // tile

    def body(c, *refs):
        o = refs[-1]
        for block in range(blocks):

            @pl.when(pl.program_id(0) == block)
            def _():
                value = None
                for s in range(count):
                    other = block ^ ((1 << s) >> 1)
                    more = dot(c[:, other * width : (other + 1) * width], refs[s][0, 0], ((1,), (1,)))
                    value = more if value is None else value + more
                o[...] = value

    def weight(s):
        return pl.BlockSpec((1, 1, tile, width), lambda i, t: (i ^ ((1 << s) >> 1), s, t, 0))

    return call(
        body,
        grid=(blocks, tiles),
        in_specs=[pl.BlockSpec((rows, blocks * width), lambda i, t: (0, 0))]
        + [weight(s) for s in range(count)],
        out_specs=pl.BlockSpec((rows, tile), lambda i, t: (0, i * tiles + t)),
        out_shape=jax.ShapeDtypeStruct((rows, blocks * width), F32),
    )(cot, *[weights] * count)


def projections(core, tokens, cot, u, v):
    rows, width = tokens.shape
    rank = u.shape[1]
    tile = rows // 2

    def body(core_ref, t, c, u_ref, v_ref, kept, sent):
        low = dot(t[...], u_ref[...], ((1,), (0,)))
        back = dot(c[...], v_ref[...], ((1,), (1,)))
        first = core_ref[0] == 0
        kept[...] = jnp.where(first, low, back)
        sent[...] = jnp.where(first, back, low)

    shape = jax.ShapeDtypeStruct((rows, rank), F32)
    return call(
        body,
        grid=(rows // tile,),
        in_specs=[
            pl.BlockSpec(memory_space=pltpu.SMEM),
            pl.BlockSpec((tile, width), lambda r: (r, 0)),
            pl.BlockSpec((tile, width), lambda r: (r, 0)),
            pl.BlockSpec((width, rank), lambda r: (0, 0)),
            pl.BlockSpec((rank, width), lambda r: (0, 0)),
        ],
        out_specs=[pl.BlockSpec((tile, rank), lambda r: (r, 0))] * 2,
        out_shape=[shape, shape],
    )(core, tokens, cot, u, v)


def pieces(me, tokens, cot, blocks, part):
    rows, width = tokens.shape
    width //= blocks
    tile = rows // 2

    def body(me_ref, t, c, held, *given):
        def shard(block, x):
            start = pl.multiple_of(block * width + (me_ref[0] ^ x) * part, part)
            return t[:, pl.ds(start, part)]

        for j in range(blocks):
            held[:, 2 * j * part : (2 * j + 1) * part] = shard(j, 0)
            held[:, (2 * j + 1) * part : (2 * j + 2) * part] = shard(j, REDUCE[j])
            for at, block in enumerate((j, j ^ 1)):
                start = 2 * at * part
                given[j][:, start : start + part] = shard(block, GATHER[j])
                given[j][:, start + part : start + 2 * part] = shard(block, GATHER[j] ^ REDUCE[j])
            given[j][:, 4 * part :] = c[:, j * width : (j + 1) * width]

    widths = [2 * blocks * part] + [4 * part + width] * blocks
    return prefetched(
        body,
        me,
        (rows // tile,),
        [pl.BlockSpec((tile, blocks * width), lambda r, m: (r, 0))] * 2,
        [pl.BlockSpec((tile, w), lambda r, m: (r, 0)) for w in widths],
        [jax.ShapeDtypeStruct((rows, w), BF16) for w in widths],
        (tokens, cot),
    )


def slot_sums(me, j, tokens, cot, given, local, partners, part):
    rows = tokens.shape[0]
    width = given.shape[1] - 4 * part
    shards = width // part
    slots = 2 * local + len(partners)
    tile = width // 2
    mine = 4 * local

    def body(me_ref, *refs):
        far = refs[mine + 2 * local : -4]
        c0, c1, kept, sent = refs[-4:]
        first = list(refs[:mine]) + list(far[0::2])
        second = list(refs[mine : mine + 2 * local]) + list(far[1::2])
        value = dot(jnp.concatenate([r[...] for r in first], 1), c0[...], ((0,), (0,)))
        value = value + dot(jnp.concatenate([r[...] for r in second], 1), c1[...], ((0,), (0,)))
        for s in range(slots):
            kept[s] = value[2 * s * part : (2 * s + 1) * part]
            sent[s] = value[(2 * s + 1) * part : (2 * s + 2) * part].astype(BF16)

    def shard(block, x):
        return pl.BlockSpec((rows, part), lambda t, m: (0, block * shards + (m[0] ^ x)))

    def pair(at):
        return pl.BlockSpec((rows, 2 * part), lambda t, m: (0, at))

    in_specs, operands = [], []
    if local:
        in_specs += [shard(j, 0), shard(j, REDUCE[j]), shard(j ^ 1, 0), shard(j ^ 1, REDUCE[j])]
        in_specs += [pair(0), pair(1)]
        operands += [tokens] * 4 + [given] * 2
    for one, two in partners:
        in_specs += [pair(one[1]), pair(two[1])]
        operands += [one[0], two[0]]
    in_specs += [
        pl.BlockSpec((rows, tile), lambda t, m: (0, j * (width // tile) + t)),
        pl.BlockSpec((rows, tile), lambda t, m: (0, 4 * part // tile + t)),
    ]
    out = pl.BlockSpec((slots, part, tile), lambda t, m: (0, 0, t))
    shape = (slots, part, width)
    return prefetched(
        body,
        me,
        (width // tile,),
        in_specs,
        [out, out],
        [jax.ShapeDtypeStruct(shape, F32), jax.ShapeDtypeStruct(shape, BF16)],
        (*operands, cot, given),
    )


def all_grads(kept, got, scale):
    blocks = len(kept)
    counts = [k.shape[0] for k in kept[0]]
    _, part, width = kept[0][0].shape
    slots = sum(counts)
    tile = width // 4

    def body(*refs):
        o = refs[-1]
        refs = iter(refs)
        for j in range(blocks):
            at = 0
            for count in counts:
                mine, theirs = next(refs), next(refs)
                for s in range(count):
                    o[:, at + s, j, :] = (mine[s] + theirs[s].astype(F32)) * scale
                at += count

    operands = [
        x for j in range(blocks) for pair in zip(kept[j], got[j]) for x in pair
    ]
    out = call(
        body,
        grid=(width // tile,),
        in_specs=[pl.BlockSpec((x.shape[0], part, tile), lambda t: (0, 0, t)) for x in operands],
        out_specs=pl.BlockSpec((part, slots, blocks, tile), lambda t: (0, 0, 0, t)),
        out_shape=jax.ShapeDtypeStruct((part, slots, blocks, width), F32),
    )(*operands)
    return jnp.transpose(out, (0, 2, 1, 3))


def gathered(given, width):
    rows = given[0].shape[0]

    def body(*refs):
        for j in range(len(given)):

            @pl.when(pl.program_id(0) == j)
            def _():
                refs[-1][...] = refs[j][...]

    return call(
        body,
        grid=(len(given),),
        in_specs=[pl.BlockSpec((rows, width), lambda j: (0, 0)) for _ in given],
        out_specs=pl.BlockSpec((rows, width), lambda j: (0, j)),
        out_shape=jax.ShapeDtypeStruct((rows, len(given) * width), BF16),
    )(*given)


def joined(base, near, low_back, u):
    rows, width = base.shape
    tile = width // 4
    skipped = (near.shape[1] - width) // tile

    def body(b, n, l, u_ref, o):
        o[...] = b[...] + n[...].astype(F32) + dot(l[...], u_ref[...], ((1,), (1,)))

    block = pl.BlockSpec((rows, tile), lambda t: (0, t))
    return call(
        body,
        grid=(width // tile,),
        in_specs=[
            block,
            pl.BlockSpec((rows, tile), lambda t: (0, skipped + t)),
            pl.BlockSpec(low_back.shape, lambda t: (0, 0)),
            pl.BlockSpec((tile, u.shape[1]), lambda t: (t, 0)),
        ],
        out_specs=block,
        out_shape=jax.ShapeDtypeStruct(base.shape, F32),
    )(base, near, low_back, u)


def added(base, terms, first):
    rows, width = terms[0].shape
    tile = rows // 4 if rows > 256 else rows

    def body(b, *refs):
        value = b[...]
        for ref in refs[:-1]:
            value = value + ref[...].astype(F32)
        refs[-1][...] = value

    block = pl.BlockSpec((tile, width), lambda r: (r + first // tile, 0))
    return call(
        body,
        grid=(rows // tile,),
        in_specs=[block] + [pl.BlockSpec((tile, width), lambda r: (r, 0)) for _ in terms],
        out_specs=block,
        out_shape=jax.ShapeDtypeStruct(base.shape, F32),
        input_output_aliases={0: 0},
    )(base, *terms)


def summed_rows(terms, before):
    me = lax.axis_index("dp")
    size = terms[0].shape[0] // 4
    parts = [
        [lax.dynamic_slice_in_dim(t, (me ^ x) * size, size, 0) for x in range(4)] for t in terms
    ]
    got = [
        swap(jnp.concatenate([p[1 + k], p[3]], 0).astype(BF16), "dp", 1 + k)
        for k, p in enumerate(parts)
    ]
    got = [g.astype(F32) for g in tie(got, before[0])]
    mine = [p[0] + g[:size] for p, g in zip(parts, got)]
    theirs = [p[2 - k] + g[size:] for k, (p, g) in enumerate(zip(parts, got))]
    got = [swap(t.astype(BF16), "dp", 2 - k) for k, t in enumerate(theirs)]
    return [m + g.astype(F32) for m, g in zip(mine, tie(got, before[1]))]


def square(tokens, cotangent, blocks_w, lowrank_u, lowrank_v):
    lb, slots, bw = blocks_w.shape[:3]
    rows = tokens.shape[0]
    n_dp = lax.axis_size("dp")
    part = bw // n_dp
    scale = 1.0 / math.sqrt(rows * n_dp)
    me = jnp.reshape(lax.axis_index("dp"), (1,)).astype(jnp.int32)
    mp_me = lax.axis_index("mp")
    core, side = mp_me & 1, mp_me >> 1 & 1
    half, cut = rows // 2, rows // 12 * 11
    near, far = 2, (3, 4)
    apart = {s: (1 << (s - 1)) // lb for s in (near, *far)}

    held, *given = pieces(me, tokens, cotangent, lb, part)
    given = [swap(g, "dp", GATHER[j]) for j, g in enumerate(given)]
    held_in = {s: swap(held, "mp", apart[s]) for s in far}

    tokens1, cot1 = tie((tokens, cotangent), held)
    kept, sent = projections(
        jnp.reshape(core, (1,)).astype(jnp.int32), tokens1, cot1, lowrank_u, lowrank_v
    )
    got = swap(sent, "mp", 1)
    cot1 = tie(cot1, kept)
    out = {near: partner_term(cot1, blocks_w, near)}
    kept = kept + tie(got, out)
    for s in far:
        cot1 = tie(cot1, out)
        out[s] = partner_term(cot1, blocks_w, s, cut)
    base = own_terms(tie(cot1, out), blocks_w, 2)
    kept = tie(kept, base)
    sent = lax.dynamic_slice_in_dim(kept, (1 - side) * half, half, 0)
    kept = lax.dynamic_slice_in_dim(kept, side * half, half, 0)
    got = swap(sent, "mp", 2)

    near_out = jnp.concatenate([held, out[near]], 1)
    given = tie(given, base)
    more = gathered(given, 2 * part)
    given, held_in, out, near_out, got, more = tie((given, held_in, out, near_out, got, more))
    more_in = {3: swap(more, "mp", apart[3])}
    kept = kept + got
    got = swap(kept, "mp", 4)
    near_out, near_more = tie((near_out, more), kept)
    near_in = swap(near_out, "mp", apart[near])
    near_more = swap(near_more, "mp", apart[near])
    got, more4 = tie((got, more))
    more_in[4] = swap(more4, "mp", apart[4])

    kept = (kept + got).astype(BF16)
    got = swap(kept, "mp", 2)
    got, near_in, near_more = tie((got, near_in, near_more))
    whole = ordered(kept, got, side, 0)
    other = swap(whole, "mp", 1)
    low_in = jnp.where(core == 0, whole, other)
    low_back = jnp.where(core == 0, other, whole)

    out = tie(out, near_more, near_in)
    more_in[3], first = tie((more_in[3], out[3][0]))
    far_in = [swap(first, "mp", apart[3]), swap(out[4][0], "mp", apart[4])]

    sums, tokens1 = [], tokens
    for j in range(lb):
        partners = [(near_in, near_more)] + [(held_in[s], more_in[s]) for s in far]
        partners = [((one, j), (two, j)) for one, two in partners]
        sums.append(slot_sums(me, j, tokens1, cotangent, given[j], True, partners, part))
    sums_in = [swap(sums[j][1], "dp", REDUCE[j]) for j in range(lb)]

    full = joined(base, near_in, low_back, lowrank_u)
    sums_in = tie(sums_in, full)
    grad_blocks = all_grads([[s[0]] for s in sums], [[s] for s in sums_in], scale)

    u_term = dot(tokens, low_back, ((0,), (0,)))
    v_term = dot(cotangent, low_in, ((0,), (0,)))
    grad_u, grad_v = summed_rows([u_term, v_term], (full, grad_blocks))
    grad_u, grad_v = grad_u * scale, grad_v.T * scale
    last_in = [swap(out[s][1], "mp", apart[s]) for s in far]
    far_in, full = tie((far_in, full), grad_blocks)
    full = added(full, far_in, 0)
    last_in = tie(last_in, full)
    grad_tokens = added(full, last_in, cut)
    return (grad_tokens, grad_blocks, grad_u, grad_v)


def general(tokens, cotangent, blocks_w, lowrank_u, lowrank_v):
    lb, slots, bw = blocks_w.shape[:3]
    rows = tokens.shape[0]
    n_dp = lax.axis_size("dp")
    part = bw // n_dp
    scale = 1.0 / math.sqrt(rows * n_dp)

    def blocks_of(value):
        return value.reshape(value.shape[0], lb, -1)

    def partner(value, slot):
        distance = (1 << slot) >> 1
        if distance < lb:
            return jnp.stack([value[:, j ^ distance] for j in range(lb)], 1)
        return swap(value, "mp", distance // lb)

    low = dot(tokens, lowrank_u, ((1,), (0,)))
    back = dot(cotangent, lowrank_v, ((1,), (1,)))
    low, back = lax.psum((low, back), "mp")
    low, back = low.astype(BF16), back.astype(BF16)

    turned = tokens.reshape(rows, lb, n_dp, part)
    turned = lax.all_to_all(turned, "dp", 2, 0, tiled=True).reshape(n_dp * rows, lb, part)
    cot_all = blocks_of(lax.all_gather(cotangent, "dp", tiled=True))
    cot = blocks_of(cotangent)
    total = blocks_of(dot(back, lowrank_u, ((1,), (1,))))
    grads = []
    for s in range(slots):
        term = jnp.einsum("tbo,bio->tbi", cot, blocks_w[:, s], preferred_element_type=F32)
        if (1 << s) >> 1 >= lb:
            term = term.astype(BF16)
        total = total + partner(term, s).astype(F32)
        grads.append(
            jnp.einsum("tbi,tbo->ibo", partner(turned, s), cot_all, preferred_element_type=F32)
        )
    grad_blocks = jnp.stack(grads, 2) * scale
    u_term = dot(tokens, back, ((0,), (0,)))
    v_term = dot(low, cotangent, ((0,), (0,)))
    grad_u = lax.psum_scatter(u_term, "dp", scatter_dimension=0, tiled=True)
    grad_v = lax.psum_scatter(v_term, "dp", scatter_dimension=1, tiled=True)
    return (total.reshape(rows, lb * bw), grad_blocks, grad_u * scale, grad_v * scale)


def per_device(tokens, cotangent, blocks_w, lowrank_u, lowrank_v):
    sizes = (blocks_w.shape[0], lax.axis_size("dp"), lax.axis_size("mp"))
    plan = square if sizes == (2, 4, 8) and blocks_w.shape[1] == 5 else general
    return plan(tokens, cotangent, blocks_w, lowrank_u, lowrank_v)


def solution(mesh):
    in_specs = (
        P("dp", "mp"),
        P("dp", "mp"),
        P("mp", None, None, None),
        P("mp", None),
        P(None, "mp"),
    )
    out_specs = (
        P("dp", "mp"),
        P("dp", "mp", None, None),
        P(("mp", "dp"), None),
        P(None, ("mp", "dp")),
    )
    return jax.shard_map(
        per_device, mesh=mesh, in_specs=in_specs, out_specs=out_specs, check_vma=False
    )
```
